256 devices in a mesh: seq: 64 (over y, z, core), ch: 4 (over x).
Axes of the slice: x: 4, y: 4, z: 8, core: 2. Of those that a mesh axis runs over, the one named last changes fastest.
Arguments:
- features: bfloat16 [3, 16384, 4096], P(None, 'seq', 'ch'), may hold values from -6 to 6
- short_taps: float32 [3, 3, 4096], P(None, None, 'ch'), may hold values from -3 to 3
- filter_taps: float32 [16384, 4096], P('seq', 'ch'), may hold values from -1.1 to 1.1, as said below
- skip_bias: float32 [4096], P('ch'), may hold values from -4 to 4
- out_weight: bfloat16 [4096, 4096], P('ch', 'seq'), may hold values from -0.09375 to 0.09375
Outputs:
- projected: bfloat16 [16384, 4096], P('seq', 'ch')
The draws below stay inside these ranges and needn't reach their ends.
Inputs may be any that keep to these rules, and one draw needn't show every extreme that they name: `filter_taps`: the long filter's taps.
All inputs are finite; a program needn't handle non-finite values.
Results may differ from the reference program's by a relative error of at most 0.0049.
Values may be sent and summed in bfloat16 or wider, within the bound.
A program may use at most 128 MiB of HBM per device.

```python
import math
import jax
import jax.numpy as jnp
from jax import lax

D = 4096
SEQ_LEN = 16384


def draw_filter_taps(key, part):
    length = SEQ_LEN
    chan_width = D
    rate_key, noise_key = jax.random.split(jax.random.fold_in(key, 11))
    low_log = math.log(1.0 / (4.0 * length))
    high_log = math.log(1.0 / 30.0)
    noise_field = jax.random.truncated_normal(noise_key, -4.0, 4.0, (length, chan_width), jnp.float32)
    decay_rate = jnp.exp(jax.random.uniform(rate_key, (chan_width,), jnp.float32, low_log, high_log))
    positions = lax.broadcasted_iota(jnp.float32, (length, chan_width), 0)
    return noise_field * jnp.exp(-positions * decay_rate[None, :]) * jnp.sqrt(2.0 * decay_rate[None, :])


def shard_levels(key, extent, shards, smallest, high):
    level = 1.0
    for position, blocks in shards:
        steps = jax.random.uniform(jax.random.fold_in(jax.random.fold_in(key, 6), position), (blocks,), jnp.float32, smallest / len(shards), high / len(shards))
        level = level * jnp.repeat(jnp.exp(steps), extent[position] // blocks).reshape((-1,) + (1,) * (len(extent) - 1 - position))
    return level


def scatter_about(rng, shape, width, reach, pieces=(), held_as=jnp.bfloat16):
    entries = jax.random.normal(rng, shape, jnp.float32) * width
    if len(pieces) > 0:
        entries = shard_levels(rng, shape, pieces, -0.22, 0.18) * entries
    return jnp.clip(entries, min=-reach, max=reach).astype(held_as)


def setup_inputs(seed: int = 0) -> dict:
    key_list = jax.random.split(jax.random.key(seed), 6)
    return {
        "features": scatter_about(key_list[0], (3, SEQ_LEN, D), 1.0, 6.0, ((1, 64), (2, 4))),
        "short_taps": scatter_about(key_list[1], (3, 3, D), 0.6, 3.0, ((2, 4),), jnp.float32),
        "filter_taps": draw_filter_taps(jax.random.fold_in(key_list[5], 71), 0),
        "skip_bias": scatter_about(key_list[3], (D,), 1.0, 4.0, ((0, 4),), jnp.float32),
        "out_weight": scatter_about(key_list[4], (D, D), D ** -0.5, 0.09375, ((0, 4), (1, 64))),
    }


def group_mix(group_args):
    feature_groups, tap_groups, filter_groups, bias_groups = group_args
    floats = feature_groups.astype(jnp.float32)
    length = floats.shape[1]
    padded = jnp.pad(floats, ((0, 0), (2, 0), (0, 0)))
    mixed = tap_groups[:, 0, None, :] * padded[:, 2:] + tap_groups[:, 1, None, :] * padded[:, 1:length + 1] + tap_groups[:, 2, None, :] * padded[:, :length]
    query_part = mixed[0]
    gated_rows = mixed[1] * mixed[2]
    fft_size = 2 * length
    spectrum = jnp.fft.rfft(gated_rows, n=fft_size, axis=0) * jnp.fft.rfft(filter_groups, n=fft_size, axis=0)
    long_part = jnp.fft.irfft(spectrum, n=fft_size, axis=0)[:length]
    return (query_part * (long_part + bias_groups[None, :] * gated_rows)).astype(jnp.bfloat16)


def reference(features, short_taps, filter_taps, skip_bias, out_weight):
    chan_width = features.shape[2]
    length = features.shape[1]
    group_width = 256 if chan_width % 256 == 0 else chan_width
    group_count = chan_width // group_width
    feature_groups = features.reshape(3, length, group_count, group_width).transpose(2, 0, 1, 3)
    tap_groups = short_taps.reshape(3, 3, group_count, group_width).transpose(2, 0, 1, 3)
    filter_groups = filter_taps.reshape(length, group_count, group_width).transpose(1, 0, 2)
    bias_groups = skip_bias.reshape(group_count, group_width)
    mixed_out = lax.map(group_mix, (feature_groups, tap_groups, filter_groups, bias_groups))
    hyena_out = mixed_out.transpose(1, 0, 2).reshape(length, chan_width)
    projected = jnp.dot(hyena_out.astype(jnp.float32), out_weight.astype(jnp.float32), precision=lax.Precision.HIGHEST)
    return projected.astype(jnp.bfloat16)
```

```python
import functools
import math

import jax
import jax.numpy as jnp
import numpy as np
from jax import lax
from jax.experimental import pallas as pl
from jax.experimental.pallas import tpu as pltpu
from jax.sharding import PartitionSpec as P

MESH = pl.DeviceIdType.MESH
f32, bf16 = jnp.float32, jnp.bfloat16

BLOCKS = 64
ROWS = 256
CHAN = 1024
SHARE = CHAN // BLOCKS
POINTS = 2 * BLOCKS * ROWS
HALF = BLOCKS + 1
PADDED = 80
GROUP = 4


def split_np(table):
    high = np.asarray(table, np.float32).astype(jnp.bfloat16)
    low = (np.asarray(table, np.float64) - high.astype(np.float64)).astype(jnp.bfloat16)
    return high, low


@functools.lru_cache(maxsize=None)
def fourier_tables():
    outer = 2 * np.pi * np.outer(np.arange(HALF), np.arange(BLOCKS)) / (2 * BLOCKS)
    block_forward = np.zeros((2 * PADDED, BLOCKS))
    block_forward[:HALF] = np.cos(outer)
    block_forward[PADDED : PADDED + HALF] = -np.sin(outer)
    weight = np.full((HALF, 1), 2.0 / POINTS)
    weight[0] = weight[-1] = 1.0 / POINTS
    block_inverse = np.zeros((BLOCKS, 2 * PADDED))
    block_inverse[:, :HALF] = (np.cos(outer) * weight).T
    block_inverse[:, PADDED : PADDED + HALF] = -(np.sin(outer) * weight).T
    twist = 2 * np.pi * np.outer(np.arange(PADDED), np.arange(ROWS)) / POINTS
    inner = 2 * np.pi * (np.outer(np.arange(ROWS), np.arange(ROWS)) % ROWS) / ROWS
    cos_in, sin_in = np.cos(inner), np.sin(inner)
    row_forward = np.block([[cos_in, -sin_in], [sin_in, cos_in]])
    row_inverse = np.block([[cos_in, sin_in], [-sin_in, cos_in]])
    return (
        *split_np(block_forward),
        *split_np(block_inverse),
        *split_np(row_forward),
        *split_np(row_inverse),
        np.cos(twist).astype(np.float32),
        np.sin(twist).astype(np.float32),
    )


def split(value):
    high = value.astype(bf16)
    return high, (value - high.astype(f32)).astype(bf16)


def dot(left, right):
    return jnp.dot(left, right, preferred_element_type=f32)


def dot_wide(left, right_high, right_low):
    high, low = split(left)
    return dot(high, right_high) + (dot(high, right_low) + dot(low, right_high))


def kernel(
    feat, taps, filt, skip, weight,
    bf_hi, bf_lo, bi_hi, bi_lo, rf_hi, rf_lo, ri_hi, ri_lo, tw_cos, tw_sin,
    out,
    halo, f_out, g_out, y_out, f_in, g_in, y_in, wide, spec, query, gated, w_own, w_all, hyena, acc,
    halo_sems, f_sems, g_sems, y_sems, t_sems, z_send, z_recv, v_send, v_recv, p_send, p_recv, h_send, h_recv,
):
    me = lax.axis_index("seq")
    col = lax.axis_index("ch")
    row = lax.div(me, 16)
    deep = lax.div(lax.rem(me, 16), 2)
    core = lax.rem(me, 2)

    def seq_at(r, d, c):
        return (r * 8 + d) * 2 + c

    def wrap(i, n):
        return lax.rem(i + n, n)

    def remote(src, dst, send, recv, **where):
        return pltpu.make_async_remote_copy(
            src_ref=src, dst_ref=dst, send_sem=send, recv_sem=recv, device_id=where, device_id_type=MESH
        )

    barrier = pltpu.get_barrier_semaphore()

    def greet(k, carry):
        pl.semaphore_signal(
            barrier, inc=1, device_id={"seq": lax.rem(me + k, BLOCKS)}, device_id_type=MESH
        )
        return carry

    lax.fori_loop(1, BLOCKS, greet, 0)
    for step in (1, 3):
        pl.semaphore_signal(barrier, inc=1, device_id={"ch": lax.rem(col + step, 4)}, device_id_type=MESH)
    mirror = {"seq": seq_at(col, deep, core), "ch": row}

    @pl.when(row != col)
    def _():
        pl.semaphore_signal(barrier, inc=1, device_id=mirror, device_id_type=MESH)

    pl.semaphore_wait(barrier, BLOCKS + 1 + (row != col).astype(jnp.int32))

    halo_copy = remote(
        feat.at[:, pl.ds(ROWS - 16, 16), :], halo, halo_sems.at[0], halo_sems.at[1],
        seq=lax.rem(me + 1, BLOCKS),
    )
    halo_copy.start()

    w_own[...] = weight[...].astype(f32).T.astype(bf16)
    mirror_copy = remote(w_own, w_all.at[col, deep, core], t_sems.at[0], t_sems.at[1], **mirror)

    @pl.when(row != col)
    def _():
        mirror_copy.start()

    @pl.when(row == col)
    def _():
        w_all[row, deep, core] = w_own[...]

    def exchange(src, dst, sems):
        def send(k, carry):
            to = lax.rem(me + k * STRIDE, BLOCKS)
            remote(
                src.at[pl.ds(pl.multiple_of(to * SHARE, SHARE), SHARE)],
                dst.at[pl.ds(pl.multiple_of(me * SHARE, SHARE), SHARE)],
                sems.at[0], sems.at[1], seq=to,
            ).start()
            return carry

        lax.fori_loop(1, BLOCKS, send, 0)
        here = pl.ds(pl.multiple_of(me * SHARE, SHARE), SHARE)
        dst[here, :] = src[here, :]

    def exchanged(src, dst, sems):
        others = pl.ds(0, (BLOCKS - 1) * SHARE)
        pltpu.make_async_copy(src.at[others], dst.at[others], sems.at[1]).wait()
        pltpu.make_async_copy(src.at[others], dst.at[others], sems.at[0]).wait()

    f_out[...] = filt[...].T.astype(bf16)
    exchange(f_out, f_in, f_sems)

    def z_copies(i):
        rows = (pl.ds(0, 64), pl.ds(0, 64)) if i < 3 else (pl.ds(0, 32), pl.ds(32, 32))
        up, down = wrap(deep - i, 8), lax.rem(deep + i, 8)
        return (
            remote(
                w_all.at[row, up, core, rows[0]], w_all.at[row, up, core, rows[0]],
                z_send.at[0, i], z_recv.at[0, i], seq=seq_at(row, lax.rem(deep + 1, 8), core),
            ),
            remote(
                w_all.at[row, down, core, rows[1]], w_all.at[row, down, core, rows[1]],
                z_send.at[1, i], z_recv.at[1, i], seq=seq_at(row, lax.rem(deep + 7, 8), core),
            ),
        )

    @pl.when(row != col)
    def _():
        mirror_copy.wait()

    z_steps = [z_copies(i) for i in range(4)]
    for copy in z_steps[0]:
        copy.start()

    halo_copy.wait()
    first = (me != 0).astype(f32)

    def mixed(b):
        rows = feat[b].astype(f32)
        edge = halo[b].astype(f32) * first
        joined = jnp.concatenate([edge[8:16], rows], axis=0)
        back_one = pltpu.roll(joined, 1, 0)[8:]
        back_two = pltpu.roll(joined, 2, 0)[8:]
        return taps[b, 0:1] * rows + taps[b, 1:2] * back_one + taps[b, 2:3] * back_two

    gated[...] = mixed(1) * mixed(2)
    g_out[...] = gated[...].T.astype(bf16)
    exchange(g_out, g_in, g_sems)
    query[...] = mixed(0)

    for i in range(1, 4):
        for copy, later in zip(z_steps[i - 1], z_steps[i]):
            copy.wait_recv()
            later.start()
    for copy in z_steps[3]:
        copy.wait_recv()

    def v_copy(direction, part, source, low, n):
        ref = w_all.at[source, pl.ds(low, n), core]
        to = lax.rem(row + (1 if direction == 0 else 3), 4)
        return remote(
            ref, ref, v_send.at[direction, part], v_recv.at[direction, part], seq=seq_at(to, deep, core)
        )

    before, after = wrap(row - 1, 4), lax.rem(row + 1, 4)
    v_up = [v_copy(0, 0, row, 0, 4), v_copy(0, 1, row, 4, 4), v_copy(0, 2, before, 0, 4)]
    v_down = [v_copy(1, 0, row, 4, 4), v_copy(1, 1, row, 0, 4), v_copy(1, 2, after, 4, 4)]
    for part in (0, 1):
        v_up[part].start()
        v_down[part].start()

    def p_copy(i):
        ref = w_all.at[lax.rem(row + i, 4), :, core]
        return remote(ref, ref, p_send.at[i], p_recv.at[i], seq=seq_at(row, deep, 1 - core))

    p_copies = [p_copy(i) for i in range(4)]
    p_copies[0].start()

    def widen(received):
        wide[0] = received[:, :128].astype(f32)
        wide[1] = received[:, 128:].astype(f32)

    def spectra(q):
        lines = []
        for c in range(GROUP):
            every = pl.ds(q * GROUP + c, BLOCKS, stride=SHARE)
            line = jnp.concatenate([wide[0, every, :], wide[1, every, :]], axis=1).astype(bf16)
            both = dot(bf_hi[...], line) + dot(bf_lo[...], line)
            real, imag = both[:PADDED], both[PADDED:]
            lines.append(
                jnp.concatenate(
                    [
                        real * tw_cos[...] + imag * tw_sin[...],
                        imag * tw_cos[...] - real * tw_sin[...],
                    ],
                    axis=1,
                )
            )
        return dot_wide(jnp.concatenate(lines, axis=0), rf_hi[...], rf_lo[...])

    exchanged(f_out, f_in, f_sems)
    widen(f_in)

    def filter_group(q, carry):
        spec[q] = spectra(q)
        return carry

    lax.fori_loop(0, SHARE // GROUP, filter_group, 0)

    v_up[0].wait_recv()
    v_up[2].start()
    v_down[0].wait_recv()
    v_down[2].start()

    exchanged(g_out, g_in, g_sems)
    widen(g_in)

    def conv_group(q, carry):
        signal = spectra(q)
        taps_spec = spec[q]
        sr, si = signal[:, :ROWS], signal[:, ROWS:]
        tr, ti = taps_spec[:, :ROWS], taps_spec[:, ROWS:]
        joint = jnp.concatenate([sr * tr - si * ti, sr * ti + si * tr], axis=1)
        back = dot_wide(joint, ri_hi[...], ri_lo[...])
        for c in range(GROUP):
            real = back[c * PADDED : (c + 1) * PADDED, :ROWS]
            imag = back[c * PADDED : (c + 1) * PADDED, ROWS:]
            both = jnp.concatenate(
                [
                    real * tw_cos[...] - imag * tw_sin[...],
                    imag * tw_cos[...] + real * tw_sin[...],
                ],
                axis=0,
            )
            high, low = split(both)
            series = dot(bi_hi[...], high) + (dot(bi_hi[...], low) + dot(bi_lo[...], high))
            every = pl.ds(q * GROUP + c, BLOCKS, stride=SHARE)
            wide[0, every, :] = series[:, :128]
            wide[1, every, :] = series[:, 128:]
        return carry

    lax.fori_loop(0, SHARE // GROUP, conv_group, 0)
    y_out[:, :128] = wide[0].astype(bf16)
    y_out[:, 128:] = wide[1].astype(bf16)
    exchange(y_out, y_in, y_sems)

    v_up[1].wait_recv()
    p_copies[3].start()
    v_down[1].wait_recv()
    p_copies[1].start()
    v_up[2].wait_recv()
    v_down[2].wait_recv()
    p_copies[2].start()

    exchanged(y_out, y_in, y_sems)
    long_conv = y_in[...].astype(f32).T
    hyena[col] = (query[...] * (long_conv + skip[...] * gated[...])).astype(bf16)

    def h_copy(direction, part, source, low):
        ref = hyena.at[source, pl.ds(low, 128)]
        to = lax.rem(col + (1 if direction == 0 else 3), 4)
        return remote(ref, ref, h_send.at[direction, part], h_recv.at[direction, part], ch=to)

    left, right = wrap(col - 1, 4), lax.rem(col + 1, 4)
    h_up = [h_copy(0, 0, col, 0), h_copy(0, 1, col, 128), h_copy(0, 2, left, 0)]
    h_down = [h_copy(1, 0, col, 128), h_copy(1, 1, col, 0), h_copy(1, 2, right, 128)]
    for part in (0, 1):
        h_up[part].start()
        h_down[part].start()
    for copy in p_copies:
        copy.wait_recv()

    def project(source, start):
        def tile(j, carry):
            cols = pl.ds(pl.multiple_of(j * 256, 256), 256)
            block = w_all[source, pl.ds(2 * j, 2)].reshape(256, CHAN)
            part = lax.dot_general(
                hyena[source], block, (((1,), (1,)), ((), ())), preferred_element_type=f32
            )
            acc[:, cols] = part if start else acc[:, cols] + part
            return carry

        lax.fori_loop(0, 4, tile, 0)

    h_up[0].wait_recv()
    h_up[2].start()
    h_down[0].wait_recv()
    h_down[2].start()
    project(col, True)
    h_up[1].wait_recv()
    project(left, False)
    h_down[1].wait_recv()
    project(right, False)
    h_up[2].wait_recv()
    h_down[2].wait_recv()
    project(lax.rem(col + 2, 4), False)
    out[...] = acc[...].astype(bf16)

    for copies in (*z_steps, v_up, v_down, p_copies, h_up, h_down):
        for copy in copies:
            copy.wait_send()


STRIDE = 1


def shards(features, short_taps, filter_taps, skip_bias, out_weight):
    tables = [jnp.asarray(t) for t in fourier_tables()]
    whole = pl.BlockSpec(memory_space=pltpu.VMEM)
    dma = pltpu.SemaphoreType.DMA
    return pl.pallas_call(
        kernel,
        out_shape=jax.ShapeDtypeStruct((ROWS, CHAN), bf16),
        in_specs=[whole] * (5 + len(tables)),
        out_specs=whole,
        scratch_shapes=[
            pltpu.VMEM((3, 16, CHAN), bf16),
            *[pltpu.VMEM((CHAN, ROWS), bf16)] * 6,
            pltpu.VMEM((2, CHAN, 128), f32),
            pltpu.VMEM((SHARE // GROUP, GROUP * PADDED, 2 * ROWS), f32),
            pltpu.VMEM((ROWS, CHAN), f32),
            pltpu.VMEM((ROWS, CHAN), f32),
            pltpu.VMEM((BLOCKS, CHAN), bf16),
            pltpu.VMEM((4, 8, 2, 64, CHAN), bf16),
            pltpu.VMEM((4, ROWS, CHAN), bf16),
            pltpu.VMEM((ROWS, CHAN), f32),
            *[dma((2,))] * 5,
            dma((2, 4)), dma((2, 4)),
            dma((2, 3)), dma((2, 3)),
            dma((4,)), dma((4,)),
            dma((2, 3)), dma((2, 3)),
        ],
        compiler_params=pltpu.CompilerParams(
            collective_id=0, has_side_effects=True, vmem_limit_bytes=60 * 1024 * 1024
        ),
    )(features, short_taps, filter_taps, skip_bias[None, :], out_weight, *tables)


def solution(mesh):
    placed = (P(None, "seq", "ch"), P(None, None, "ch"), P("seq", "ch"), P("ch"), P("ch", "seq"))
    return jax.shard_map(
        shards, mesh=mesh, in_specs=placed, out_specs=P("seq", "ch"), check_vma=False
    )
```

```python
import functools
import math

import jax
import jax.numpy as jnp
import numpy as np
from jax import lax
from jax.experimental import pallas as pl
from jax.experimental.pallas import tpu as pltpu
from jax.sharding import PartitionSpec as P

MESH = pl.DeviceIdType.MESH
f32, bf16 = jnp.float32, jnp.bfloat16

BLOCKS = 64
ROWS = 256
CHAN = 1024
SHARE = CHAN // BLOCKS
POINTS = 2 * BLOCKS * ROWS
GROUP = 4


def split_np(table):
    high = np.asarray(table, np.float32).astype(jnp.bfloat16)
    low = (np.asarray(table, np.float64) - high.astype(np.float64)).astype(jnp.bfloat16)
    return high, low


@functools.lru_cache(maxsize=None)
def fourier_tables():
    steps = np.arange(BLOCKS) + 0.5
    outer = 2 * np.pi * np.outer(steps, np.arange(BLOCKS)) / (2 * BLOCKS)
    block_forward = np.concatenate([np.cos(outer), -np.sin(outer)], axis=0)
    block_inverse = block_forward.T * (2.0 / POINTS)
    twist = 2 * np.pi * np.outer(steps, np.arange(ROWS)) / POINTS
    inner = 2 * np.pi * (np.outer(np.arange(ROWS), np.arange(ROWS)) % ROWS) / ROWS
    cos_in, sin_in = np.cos(inner), np.sin(inner)
    row_forward = np.block([[cos_in, -sin_in], [sin_in, cos_in]])
    row_inverse = np.block([[cos_in, sin_in], [-sin_in, cos_in]])
    return (
        np.concatenate(split_np(block_forward), axis=1),
        *split_np(block_inverse),
        np.cos(twist).astype(np.float32),
        np.sin(twist).astype(np.float32),
        np.stack(split_np(row_forward) + split_np(row_inverse)),
    )


def split(value):
    high = value.astype(bf16)
    return high, (value - high.astype(f32)).astype(bf16)


def dot(left, right):
    return jnp.dot(left, right, preferred_element_type=f32)


def dot_wide(left, right_high, right_low):
    high, low = split(left)
    return dot(high, right_high) + (dot(high, right_low) + dot(low, right_high))


def kernel(
    feat_far, filt_far, weight_far, row_far, taps, skip, bf, bi_hi, bi_lo, tw_cos, tw_sin,
    out,
    feat, filt, rows, halo, f_out, g_out, f_in, g_in, y_out, y_in,
    wide, spec, query, gated, w_all, hyena, acc,
    load_sems, greet_sems, halo_sems, f_sems, g_sems, y_sems, t_sems,
    z_send, z_recv, v_send, v_recv, u_send, u_recv, p_send, p_recv, h_send, h_recv,
):
    me = lax.axis_index("seq")
    col = lax.axis_index("ch")
    row = lax.div(me, 16)
    deep = lax.div(lax.rem(me, 16), 2)
    core = lax.rem(me, 2)

    def seq_at(r, d, c):
        return (r * 8 + d) * 2 + c

    def wrap(i, n):
        return lax.rem(i + n, n)

    def signal(sem, **where):
        pl.semaphore_signal(sem, inc=1, device_id=where, device_id_type=MESH)

    def remote(src, dst, send, recv, **where):
        return pltpu.make_async_remote_copy(
            src_ref=src, dst_ref=dst, send_sem=send, recv_sem=recv, device_id=where, device_id_type=MESH
        )

    barrier = pltpu.get_barrier_semaphore()
    after_me, before_me = lax.rem(me + 1, BLOCKS), wrap(me - 1, BLOCKS)
    mirror = {"seq": seq_at(col, deep, core), "ch": row}
    signal(barrier, seq=seq_at(row, deep, 1 - core))
    signal(barrier, seq=jnp.where(core == 0, before_me, after_me))
    for step in range(1, 8):
        signal(barrier, seq=seq_at(row, lax.rem(deep + step, 8), core))
    for step in range(1, 4):
        signal(barrier, seq=seq_at(lax.rem(row + step, 4), deep, core))
    for step in (1, 3):
        signal(barrier, ch=lax.rem(col + step, 4))

    @pl.when(row != col)
    def _():
        signal(barrier, **mirror)

    loads = [
        pltpu.make_async_copy(far, near, load_sems.at[i])
        for i, (far, near) in enumerate(((filt_far, filt), (feat_far, feat), (row_far, rows)))
    ]
    for load in loads:
        load.start()
    loads[0].wait()
    f_out[...] = filt[...].T.astype(bf16)

    pl.semaphore_wait(barrier, 14 + (row != col).astype(jnp.int32))

    halo_copy = remote(
        feat_far.at[:, pl.ds(ROWS - 16, 16), :], halo, halo_sems.at[0], halo_sems.at[1], seq=after_me
    )
    halo_copy.start()

    mirror_copy = remote(weight_far, w_all.at[col, deep, core], t_sems.at[0], t_sems.at[1], **mirror)
    same_copy = pltpu.make_async_copy(weight_far, w_all.at[row, deep, core], t_sems.at[1])

    @pl.when(row != col)
    def _():
        mirror_copy.start()

    @pl.when(row == col)
    def _():
        same_copy.start()

    for step in range(1, 4):
        signal(greet_sems.at[0], seq=seq_at(lax.rem(row + step, 4), deep, core))
    loads[1].wait()
    first = (me != 0).astype(f32)

    def mixed(b):
        middle = feat[b].astype(f32)
        back_one = pltpu.roll(middle, 1, 0)
        back_two = pltpu.roll(middle, 2, 0)
        return taps[b, 0:1] * middle + taps[b, 1:2] * back_one + taps[b, 2:3] * back_two

    def mixed_top(b):
        top = feat[b, 0:16].astype(f32)
        joined = jnp.concatenate([halo[b].astype(f32) * first, top], axis=0)
        back_one = pltpu.roll(joined, 1, 0)[16:]
        back_two = pltpu.roll(joined, 2, 0)[16:]
        return taps[b, 0:1] * top + taps[b, 1:2] * back_one + taps[b, 2:3] * back_two

    pl.semaphore_wait(greet_sems.at[0], 3)
    signal(greet_sems.at[1], seq=seq_at(row, deep, 1 - core))
    gated[...] = mixed(1) * mixed(2)
    pl.semaphore_wait(greet_sems.at[1], 1)

    def exchange(src, dst, sems):
        def send(k, carry):
            to = lax.rem(me + k * STRIDE, BLOCKS)
            remote(
                src.at[pl.ds(pl.multiple_of(to * SHARE, SHARE), SHARE)],
                dst.at[pl.ds(pl.multiple_of(me * SHARE, SHARE), SHARE)],
                sems.at[0], sems.at[1], seq=to,
            ).start()
            return carry

        lax.fori_loop(1, BLOCKS, send, 0)
        here = pl.ds(pl.multiple_of(me * SHARE, SHARE), SHARE)
        dst[here, :] = src[here, :]

    def exchanged(src, dst, sems):
        others = pl.ds(0, (BLOCKS - 1) * SHARE)
        pltpu.make_async_copy(src.at[others], dst.at[others], sems.at[1]).wait()
        pltpu.make_async_copy(src.at[others], dst.at[others], sems.at[0]).wait()

    exchange(f_out, f_in, f_sems)

    def z_copies(i):
        parts = (pl.ds(0, 64), pl.ds(0, 64)) if i < 3 else (pl.ds(0, 32), pl.ds(32, 32))
        up = w_all.at[row, wrap(deep - i, 8), core, parts[0]]
        down = w_all.at[row, lax.rem(deep + i, 8), core, parts[1]]
        return (
            remote(up, up, z_send.at[0, i], z_recv.at[0, i], seq=seq_at(row, lax.rem(deep + 1, 8), core)),
            remote(down, down, z_send.at[1, i], z_recv.at[1, i], seq=seq_at(row, lax.rem(deep + 7, 8), core)),
        )

    up_row, down_row = lax.rem(row + 1, 4), wrap(row - 1, 4)

    def v_copies(i):
        block = w_all.at[row, lax.rem(deep + i, 8), core]
        return (
            remote(block, block, v_send.at[0, i], v_recv.at[0, i], seq=seq_at(up_row, deep, core)),
            remote(block, block, v_send.at[1, i], v_recv.at[1, i], seq=seq_at(down_row, deep, core)),
        )

    def u_copy(i):
        source, to = (down_row, up_row) if i < 4 else (up_row, down_row)
        block = w_all.at[source, lax.rem(deep + i, 8), core]
        return remote(block, block, u_send.at[i], u_recv.at[i], seq=seq_at(to, deep, core))

    z_steps = [z_copies(i) for i in range(4)]
    v_steps = [v_copies(i) for i in range(8)]
    u_steps = [u_copy(i) for i in range(8)]

    def start(copies):
        for copy in copies:
            copy.start()

    def received(copies):
        for copy in copies:
            copy.wait_recv()

    @pl.when(row != col)
    def _():
        mirror_copy.wait()

    @pl.when(row == col)
    def _():
        same_copy.wait()

    start(z_steps[0])
    start(v_steps[0])

    halo_copy.wait()
    gated[0:16] = mixed_top(1) * mixed_top(2)
    g_out[...] = gated[...].T.astype(bf16)
    exchange(g_out, g_in, g_sems)
    query[...] = mixed(0)
    query[0:16] = mixed_top(0)

    for i in range(1, 4):
        received(z_steps[i - 1])
        start(z_steps[i])
        start(v_steps[i])
        start(v_steps[8 - i])
    received(z_steps[3])
    start(v_steps[4])

    def p_copy(i):
        ref = w_all.at[lax.rem(row + i, 4), :, core]
        return remote(ref, ref, p_send.at[i], p_recv.at[i], seq=seq_at(row, deep, 1 - core))

    p_copies = [p_copy(i) for i in range(4)]
    p_copies[0].start()

    def pass_on(i):
        if i < 4:
            v_steps[i][0].wait_recv()
        else:
            v_steps[i][1].wait_recv()
        u_steps[i].start()

    def widen(arrived):
        wide[0] = arrived[:, :128].astype(f32)
        wide[1] = arrived[:, 128:].astype(f32)

    def spectra(q):
        lines = []
        for c in range(GROUP):
            every = pl.ds(q * GROUP + c, BLOCKS, stride=SHARE)
            line = jnp.concatenate([wide[0, every, :], wide[1, every, :]], axis=1)
            both = dot(bf[...], jnp.concatenate([line, line], axis=0).astype(bf16))
            real, imag = both[:BLOCKS], both[BLOCKS:]
            lines.append(
                jnp.concatenate(
                    [
                        real * tw_cos[...] + imag * tw_sin[...],
                        imag * tw_cos[...] - real * tw_sin[...],
                    ],
                    axis=1,
                )
            )
        return dot_wide(jnp.concatenate(lines, axis=0), rows[0], rows[1])

    exchanged(f_out, f_in, f_sems)
    widen(f_in)
    loads[2].wait()

    def filter_group(q, carry):
        spec[q] = spectra(q)
        return carry

    lax.fori_loop(0, SHARE // GROUP, filter_group, 0)

    for i in (0, 1, 7, 2, 6):
        pass_on(i)

    exchanged(g_out, g_in, g_sems)
    widen(g_in)

    def conv_group(q, carry):
        spectrum = spectra(q)
        taps_spec = spec[q]
        sr, si = spectrum[:, :ROWS], spectrum[:, ROWS:]
        tr, ti = taps_spec[:, :ROWS], taps_spec[:, ROWS:]
        joint = jnp.concatenate([sr * tr - si * ti, sr * ti + si * tr], axis=1)
        back = dot_wide(joint, rows[2], rows[3])
        for c in range(GROUP):
            real = back[c * BLOCKS : (c + 1) * BLOCKS, :ROWS]
            imag = back[c * BLOCKS : (c + 1) * BLOCKS, ROWS:]
            both = jnp.concatenate(
                [
                    real * tw_cos[...] - imag * tw_sin[...],
                    imag * tw_cos[...] + real * tw_sin[...],
                ],
                axis=0,
            )
            high, low = split(both)
            series = dot(bi_hi[...], high) + (dot(bi_hi[...], low) + dot(bi_lo[...], high))
            every = pl.ds(q * GROUP + c, BLOCKS, stride=SHARE)
            wide[0, every, :] = series[:, :128]
            wide[1, every, :] = series[:, 128:]
        return carry

    lax.fori_loop(0, SHARE // GROUP, conv_group, 0)
    for half in range(2):
        y_out[half] = wide[half].astype(bf16)
        exchange(y_out.at[half], y_in.at[half], y_sems.at[half])

    for i in (3, 5, 4):
        pass_on(i)
    for i in range(8):
        if i < 4:
            v_steps[i][1].wait_recv()
        else:
            v_steps[i][0].wait_recv()
    p_copies[3].start()
    p_copies[1].start()

    left, right = wrap(col - 1, 4), lax.rem(col + 1, 4)

    def h_copies(half, passing):
        if passing:
            up = hyena.at[left, pl.ds(half * 128, 64)]
            down = hyena.at[right, pl.ds(half * 128 + 64, 64)]
        else:
            up = down = hyena.at[col, pl.ds(half * 128, 128)]
        i = 2 * passing + half
        return (
            remote(up, up, h_send.at[0, i], h_recv.at[0, i], ch=right),
            remote(down, down, h_send.at[1, i], h_recv.at[1, i], ch=left),
        )

    h_own = [h_copies(half, 0) for half in range(2)]
    h_far = [h_copies(half, 1) for half in range(2)]
    for half in range(2):
        exchanged(y_out.at[half], y_in.at[half], y_sems.at[half])
        part = slice(half * 128, half * 128 + 128)
        long_conv = y_in[half].astype(f32).T
        hyena[col, part] = (query[part] * (long_conv + skip[...] * gated[part])).astype(bf16)
        start(h_own[half])

    def project(source, half, fresh):
        part = slice(half * 128, half * 128 + 128)

        def tile(j, carry):
            cols = pl.ds(pl.multiple_of(j * 256, 256), 256)
            block = w_all[source, pl.ds(2 * j, 2)].reshape(256, CHAN)
            sums = lax.dot_general(
                hyena[source, part], block, (((1,), (1,)), ((), ())), preferred_element_type=f32
            )
            acc[part, cols] = sums if fresh else acc[part, cols] + sums
            return carry

        lax.fori_loop(0, 4, tile, 0)

    received(h_own[0])
    start(h_far[0])
    received(u_steps)
    p_copies[2].start()
    received(p_copies)
    project(col, 0, True)
    received(h_own[1])
    start(h_far[1])
    project(left, 0, False)
    project(right, 0, False)
    project(col, 1, True)
    received(h_far[0])
    project(lax.rem(col + 2, 4), 0, False)
    project(left, 1, False)
    project(right, 1, False)
    received(h_far[1])
    project(lax.rem(col + 2, 4), 1, False)
    out[...] = acc[...].astype(bf16)

    for copies in (*z_steps, *v_steps, u_steps, p_copies, *h_own, *h_far):
        for copy in copies:
            copy.wait_send()


STRIDE = 23


def shards(features, short_taps, filter_taps, skip_bias, out_weight):
    tables = [jnp.asarray(t) for t in fourier_tables()]
    near = pl.BlockSpec(memory_space=pltpu.VMEM)
    far = pl.BlockSpec(memory_space=pl.ANY)
    dma, vmem = pltpu.SemaphoreType.DMA, pltpu.VMEM
    return pl.pallas_call(
        kernel,
        out_shape=jax.ShapeDtypeStruct((ROWS, CHAN), bf16),
        in_specs=[far] * 4 + [near] * 7,
        out_specs=near,
        scratch_shapes=[
            vmem((3, ROWS, CHAN), bf16),
            vmem((ROWS, CHAN), f32),
            vmem((4, 2 * ROWS, 2 * ROWS), bf16),
            vmem((3, 16, CHAN), bf16),
            *[vmem((CHAN, ROWS), bf16)] * 4,
            *[vmem((2, CHAN, 128), bf16)] * 2,
            vmem((2, CHAN, 128), f32),
            vmem((SHARE // GROUP, GROUP * BLOCKS, 2 * ROWS), f32),
            vmem((ROWS, CHAN), f32),
            vmem((ROWS, CHAN), f32),
            vmem((4, 8, 2, 64, CHAN), bf16),
            vmem((4, ROWS, CHAN), bf16),
            vmem((ROWS, CHAN), f32),
            dma((3,)),
            pltpu.SemaphoreType.REGULAR((2,)),
            *[dma((2,))] * 3,
            dma((2, 2)),
            dma((2,)),
            *[dma((2, 4))] * 2,
            *[dma((2, 8))] * 2,
            *[dma((8,))] * 2,
            *[dma((4,))] * 2,
            *[dma((2, 4))] * 2,
        ],
        compiler_params=pltpu.CompilerParams(
            collective_id=0, has_side_effects=True, vmem_limit_bytes=60 * 1024 * 1024
        ),
    )(
        features, filter_taps, out_weight.T, tables[5],
        short_taps, skip_bias[None, :], *tables[:5],
    )


def solution(mesh):
    placed = (P(None, "seq", "ch"), P(None, None, "ch"), P("seq", "ch"), P("ch"), P("ch", "seq"))
    return jax.shard_map(
        shards, mesh=mesh, in_specs=placed, out_specs=P("seq", "ch"), check_vma=False
    )
```

```python
import functools
import math

import jax
import jax.numpy as jnp
import numpy as np
from jax import lax
from jax.experimental import pallas as pl
from jax.experimental.pallas import tpu as pltpu
from jax.sharding import PartitionSpec as P

MESH = pl.DeviceIdType.MESH
f32, bf16 = jnp.float32, jnp.bfloat16

BLOCKS = 64
ROWS = 256
CHAN = 1024
SHARE = CHAN // BLOCKS
POINTS = 2 * BLOCKS * ROWS
GROUP = 4
WAVE = CHAN // 2


def split_np(table):
    high = np.asarray(table, np.float32).astype(jnp.bfloat16)
    low = (np.asarray(table, np.float64) - high.astype(np.float64)).astype(jnp.bfloat16)
    return high, low


@functools.lru_cache(maxsize=None)
def fourier_tables():
    steps = np.arange(BLOCKS) + 0.5
    outer = 2 * np.pi * np.outer(steps, np.arange(BLOCKS)) / (2 * BLOCKS)
    block_forward = np.concatenate([np.cos(outer), -np.sin(outer)], axis=0)
    block_inverse = block_forward.T * (2.0 / POINTS)
    twist = 2 * np.pi * np.outer(steps, np.arange(ROWS)) / POINTS
    inner = 2 * np.pi * (np.outer(np.arange(ROWS), np.arange(ROWS)) % ROWS) / ROWS
    cos_in, sin_in = np.cos(inner), np.sin(inner)
    row_forward = np.block([[cos_in, -sin_in], [sin_in, cos_in]])
    row_inverse = np.block([[cos_in, sin_in], [-sin_in, cos_in]])
    return (
        np.concatenate(split_np(block_forward), axis=1),
        *split_np(block_inverse),
        np.cos(twist).astype(np.float32),
        np.sin(twist).astype(np.float32),
        np.stack(split_np(row_forward) + split_np(row_inverse)),
    )


def split(value):
    high = value.astype(bf16)
    return high, (value - high.astype(f32)).astype(bf16)


def dot(left, right):
    return jnp.dot(left, right, preferred_element_type=f32)


def dot_wide(left, right_high, right_low):
    high, low = split(left)
    return dot(high, right_high) + (dot(high, right_low) + dot(low, right_high))


def kernel(
    feat_far, filt_far, weight_far, row_far, taps, skip, bf, bi_hi, bi_lo, tw_cos, tw_sin,
    out,
    feat, filt, rows, halo, f_out, g_out, f_in, g_in, y_out, y_in,
    wide, spec, query, gated, w_all, hyena, acc,
    load_sems, greet_sems, halo_sems, f_sems, g_sems, y_sems, t_sems,
    z_send, z_recv, v_send, v_recv, u_send, u_recv, p_send, p_recv, h_send, h_recv,
):
    me = lax.axis_index("seq")
    col = lax.axis_index("ch")
    row = lax.div(me, 16)
    deep = lax.div(lax.rem(me, 16), 2)
    core = lax.rem(me, 2)

    def seq_at(r, d, c):
        return (r * 8 + d) * 2 + c

    def wrap(i, n):
        return lax.rem(i + n, n)

    def signal(sem, **where):
        pl.semaphore_signal(sem, inc=1, device_id=where, device_id_type=MESH)

    def remote(src, dst, send, recv, **where):
        return pltpu.make_async_remote_copy(
            src_ref=src, dst_ref=dst, send_sem=send, recv_sem=recv, device_id=where, device_id_type=MESH
        )

    barrier = pltpu.get_barrier_semaphore()
    after_me, before_me = lax.rem(me + 1, BLOCKS), wrap(me - 1, BLOCKS)
    mirror = {"seq": seq_at(col, deep, core), "ch": row}
    signal(barrier, seq=seq_at(row, deep, 1 - core))
    signal(barrier, seq=jnp.where(core == 0, before_me, after_me))
    for step in range(1, 8):
        signal(barrier, seq=seq_at(row, lax.rem(deep + step, 8), core))
    for step in range(1, 4):
        signal(barrier, seq=seq_at(lax.rem(row + step, 4), deep, core))
    for step in (1, 3):
        signal(barrier, ch=lax.rem(col + step, 4))

    @pl.when(row != col)
    def _():
        signal(barrier, **mirror)

    loads = [
        pltpu.make_async_copy(far, near, load_sems.at[i])
        for i, (far, near) in enumerate(((filt_far, filt), (feat_far, feat), (row_far, rows)))
    ]
    for load in loads:
        load.start()
    loads[0].wait()

    def packed(value, wave):
        turned = value[:, wave * WAVE : (wave + 1) * WAVE].T
        parts = [turned[:, h * 128 : (h + 1) * 128].reshape(BLOCKS, 8, 128) for h in range(2)]
        return jnp.concatenate(parts, axis=1).reshape(CHAN, 128).astype(bf16)

    f_out[0] = packed(filt[...], 0)

    pl.semaphore_wait(barrier, 14 + (row != col).astype(jnp.int32))

    halo_copy = remote(
        feat_far.at[:, pl.ds(ROWS - 16, 16), :], halo, halo_sems.at[0], halo_sems.at[1], seq=after_me
    )
    halo_copy.start()

    mirror_copy = remote(weight_far, w_all.at[col, deep, core], t_sems.at[0], t_sems.at[1], **mirror)
    same_copy = pltpu.make_async_copy(weight_far, w_all.at[row, deep, core], t_sems.at[1])

    @pl.when(row != col)
    def _():
        mirror_copy.start()

    @pl.when(row == col)
    def _():
        same_copy.start()

    def share_to(src, dst, sems, to):
        remote(
            src.at[pl.ds(pl.multiple_of(to * SHARE, SHARE), SHARE)],
            dst.at[pl.ds(pl.multiple_of(me * SHARE, SHARE), SHARE)],
            sems.at[0], sems.at[1], seq=to,
        ).start()

    def exchange(src, dst, sems, begin=1, end=BLOCKS):
        def send(k, carry):
            share_to(src, dst, sems, lax.rem(me + k * STRIDE, BLOCKS))
            return carry

        lax.fori_loop(begin, end, send, 0)
        if begin == 1:
            here = pl.ds(pl.multiple_of(me * SHARE, SHARE), SHARE)
            dst[here, :] = src[here, :]

    for step in range(1, 4):
        signal(greet_sems.at[0], seq=seq_at(lax.rem(row + step, 4), deep, core))

    def to_line(k, carry):
        share_to(f_out.at[0], f_in.at[0], f_sems.at[0], seq_at(row, lax.rem(deep + 3 * k, 8), core))
        return carry

    def to_core(k, carry):
        near_by = seq_at(lax.rem(row + 1 + lax.rem(k, 3), 4), lax.rem(deep + 3 * k, 8), core)
        share_to(f_out.at[0], f_in.at[0], f_sems.at[0], near_by)
        return carry

    def to_other(k, carry):
        at = row * 8 + deep + 11 * k
        share_to(f_out.at[0], f_in.at[0], f_sems.at[0], lax.rem(at, 32) * 2 + 1 - core)
        return carry

    lax.fori_loop(1, 8, to_line, 0)
    here = pl.ds(pl.multiple_of(me * SHARE, SHARE), SHARE)
    f_in[0, here, :] = f_out[0, here, :]
    loads[1].wait()
    first = (me != 0).astype(f32)

    def mixed(b):
        middle = feat[b].astype(f32)
        back_one = pltpu.roll(middle, 1, 0)
        back_two = pltpu.roll(middle, 2, 0)
        return taps[b, 0:1] * middle + taps[b, 1:2] * back_one + taps[b, 2:3] * back_two

    def mixed_top(b):
        top = feat[b, 0:16].astype(f32)
        joined = jnp.concatenate([halo[b].astype(f32) * first, top], axis=0)
        back_one = pltpu.roll(joined, 1, 0)[16:]
        back_two = pltpu.roll(joined, 2, 0)[16:]
        return taps[b, 0:1] * top + taps[b, 1:2] * back_one + taps[b, 2:3] * back_two

    pl.semaphore_wait(greet_sems.at[0], 3)
    signal(greet_sems.at[1], seq=seq_at(row, deep, 1 - core))
    lax.fori_loop(0, 24, to_core, 0)
    pl.semaphore_wait(greet_sems.at[1], 1)
    gated[...] = mixed(1) * mixed(2)

    def exchanged(src, dst, sems):
        others = pl.ds(0, (BLOCKS - 1) * SHARE)
        pltpu.make_async_copy(src.at[others], dst.at[others], sems.at[1]).wait()
        pltpu.make_async_copy(src.at[others], dst.at[others], sems.at[0]).wait()

    def z_copies(i):
        parts = (pl.ds(0, 64), pl.ds(0, 64)) if i < 3 else (pl.ds(0, 32), pl.ds(32, 32))
        up = w_all.at[row, wrap(deep - i, 8), core, parts[0]]
        down = w_all.at[row, lax.rem(deep + i, 8), core, parts[1]]
        return (
            remote(up, up, z_send.at[0, i], z_recv.at[0, i], seq=seq_at(row, lax.rem(deep + 1, 8), core)),
            remote(down, down, z_send.at[1, i], z_recv.at[1, i], seq=seq_at(row, lax.rem(deep + 7, 8), core)),
        )

    up_row, down_row = lax.rem(row + 1, 4), wrap(row - 1, 4)

    def v_copies(i):
        block = w_all.at[row, lax.rem(deep + i, 8), core]
        return (
            remote(block, block, v_send.at[0, i], v_recv.at[0, i], seq=seq_at(up_row, deep, core)),
            remote(block, block, v_send.at[1, i], v_recv.at[1, i], seq=seq_at(down_row, deep, core)),
        )

    def u_copy(i):
        source, to = (down_row, up_row) if i < 4 else (up_row, down_row)
        block = w_all.at[source, lax.rem(deep + i, 8), core]
        return remote(block, block, u_send.at[i], u_recv.at[i], seq=seq_at(to, deep, core))

    z_steps = [z_copies(i) for i in range(4)]
    v_steps = [v_copies(i) for i in range(8)]
    u_steps = [u_copy(i) for i in range(8)]

    def start(copies):
        for copy in copies:
            copy.start()

    def received(copies):
        for copy in copies:
            copy.wait_recv()

    def p_copy(i, slot):
        ref = w_all.at[lax.rem(row + i, 4), lax.rem(deep + slot, 8), core]
        return remote(ref, ref, p_send.at[i, slot], p_recv.at[i, slot], seq=seq_at(row, deep, 1 - core))

    p_copies = [[p_copy(i, slot) for slot in range(8)] for i in range(4)]

    def spread(slot):
        start(v_steps[slot])
        p_copies[0][slot].start()

    def take_lines(slot):
        v_steps[slot][0].wait_recv()
        if slot < 4:
            u_steps[slot].start()
        p_copies[3][slot].start()
        v_steps[slot][1].wait_recv()
        if slot >= 4:
            u_steps[slot].start()
        p_copies[1][slot].start()

    lax.fori_loop(0, 32, to_other, 0)
    f_out[1] = packed(filt[...], 1)

    halo_copy.wait()
    gated[0:16] = mixed_top(1) * mixed_top(2)
    for wave in range(2):
        g_out[wave] = packed(gated[...], wave)

    def share(src, dst, sems, wave, begin=1, end=BLOCKS):
        exchange(src.at[wave], dst.at[wave], sems.at[wave], begin, end)

    share(g_out, g_in, g_sems, 0)

    @pl.when(row != col)
    def _():
        mirror_copy.wait()

    @pl.when(row == col)
    def _():
        same_copy.wait()

    start(z_steps[0])
    spread(0)
    share(f_out, f_in, f_sems, 1)
    query[...] = mixed(0)
    query[0:16] = mixed_top(0)
    received(z_steps[0])
    start(z_steps[1])
    spread(1)
    spread(7)
    share(g_out, g_in, g_sems, 1)

    def spectra(wave, q):
        lines = []
        for c in range(GROUP):
            line = jnp.concatenate([wide[wave, every, :] for every in every_block(q, c)], axis=1)
            both = dot(bf[...], jnp.concatenate([line, line], axis=0).astype(bf16))
            real, imag = both[:BLOCKS], both[BLOCKS:]
            lines.append(
                jnp.concatenate(
                    [
                        real * tw_cos[...] + imag * tw_sin[...],
                        imag * tw_cos[...] - real * tw_sin[...],
                    ],
                    axis=1,
                )
            )
        return dot_wide(jnp.concatenate(lines, axis=0), rows[0], rows[1])

    def every_block(q, c):
        return [pl.ds(q * GROUP + c + 8 * h, BLOCKS, stride=SHARE) for h in range(2)]

    def filter_wave(wave):
        exchanged(f_out.at[wave], f_in.at[wave], f_sems.at[wave])
        wide[wave] = f_in[wave].astype(f32)

        def filter_group(q, carry):
            spec[2 * wave + q] = spectra(wave, q)
            return carry

        lax.fori_loop(0, 2, filter_group, 0)

    def conv_wave(wave):
        exchanged(g_out.at[wave], g_in.at[wave], g_sems.at[wave])
        wide[wave] = g_in[wave].astype(f32)

        def conv_group(q, carry):
            spectrum = spectra(wave, q)
            taps_spec = spec[2 * wave + q]
            sr, si = spectrum[:, :ROWS], spectrum[:, ROWS:]
            tr, ti = taps_spec[:, :ROWS], taps_spec[:, ROWS:]
            joint = jnp.concatenate([sr * tr - si * ti, sr * ti + si * tr], axis=1)
            back = dot_wide(joint, rows[2], rows[3])
            for c in range(GROUP):
                real = back[c * BLOCKS : (c + 1) * BLOCKS, :ROWS]
                imag = back[c * BLOCKS : (c + 1) * BLOCKS, ROWS:]
                both = jnp.concatenate(
                    [
                        real * tw_cos[...] - imag * tw_sin[...],
                        imag * tw_cos[...] + real * tw_sin[...],
                    ],
                    axis=0,
                )
                high, low = split(both)
                series = dot(bi_hi[...], high) + (dot(bi_hi[...], low) + dot(bi_lo[...], high))
                for h, every in enumerate(every_block(q, c)):
                    wide[wave, every, :] = series[:, h * 128 : (h + 1) * 128]
            return carry

        lax.fori_loop(0, 2, conv_group, 0)
        y_out[wave] = wide[wave].astype(bf16)
        share(y_out, y_in, y_sems, wave)

    loads[2].wait()
    filter_wave(0)
    received(z_steps[1])
    start(z_steps[2])
    spread(2)
    spread(6)
    conv_wave(0)
    received(z_steps[2])
    start(z_steps[3])
    spread(3)
    spread(5)
    take_lines(0)
    filter_wave(1)
    received(z_steps[3])
    spread(4)
    for slot in EARLY:
        take_lines(slot)
    conv_wave(1)
    for slot in MIDDLE:
        take_lines(slot)

    left, right = wrap(col - 1, 4), lax.rem(col + 1, 4)

    def h_copies(wave, passing):
        if passing:
            up = hyena.at[left, wave, pl.ds(0, 128)]
            down = hyena.at[right, wave, pl.ds(128, 128)]
        else:
            up = down = hyena.at[col, wave]
        i = 2 * passing + wave
        return (
            remote(up, up, h_send.at[0, i], h_recv.at[0, i], ch=right),
            remote(down, down, h_send.at[1, i], h_recv.at[1, i], ch=left),
        )

    h_own = [h_copies(wave, 0) for wave in range(2)]
    h_far = [h_copies(wave, 1) for wave in range(2)]

    def finish(wave):
        exchanged(y_out.at[wave], y_in.at[wave], y_sems.at[wave])
        series = y_in[wave].astype(f32).reshape(BLOCKS, SHARE, 128)
        lanes = slice(wave * WAVE, (wave + 1) * WAVE)
        for h in range(2):
            part = slice(h * 128, h * 128 + 128)
            long_conv = series[:, 8 * h : 8 * h + 8].reshape(WAVE, 128).T
            hyena[col, wave, part] = (
                query[part, lanes] * (long_conv + skip[:, lanes] * gated[part, lanes])
            ).astype(bf16)
        start(h_own[wave])

    def project(source, wave, fresh=False):
        def tile(j, carry):
            cols = pl.ds(pl.multiple_of(j * 256, 256), 256)
            block = w_all[source, pl.ds(2 * j, 2), :, :, wave * WAVE : (wave + 1) * WAVE]
            sums = lax.dot_general(
                hyena[source, wave], block.reshape(256, WAVE), (((1,), (1,)), ((), ())),
                preferred_element_type=f32,
            )
            acc[:, cols] = sums if fresh else acc[:, cols] + sums
            return carry

        lax.fori_loop(0, 4, tile, 0)

    finish(0)
    for slot in LATE[:-1]:
        take_lines(slot)
    received(h_own[0])
    start(h_far[0])
    finish(1)
    for slot in LATE[-1:]:
        take_lines(slot)
    for slot in range(8):
        u_steps[slot].wait_recv()
        p_copies[2][slot].start()
    for copies in p_copies:
        received(copies)
    project(col, 0, True)
    received(h_own[1])
    start(h_far[1])
    project(left, 0)
    project(right, 0)
    project(col, 1)
    received(h_far[0])
    project(lax.rem(col + 2, 4), 0)
    project(left, 1)
    project(right, 1)
    received(h_far[1])
    project(lax.rem(col + 2, 4), 1)
    out[...] = acc[...].astype(bf16)

    for copies in (*z_steps, *v_steps, u_steps, *p_copies, *h_own, *h_far):
        for copy in copies:
            copy.wait_send()


STRIDE = 23
EARLY, MIDDLE, LATE = (1, 7), (2, 6), (3, 5, 4)


def shards(features, short_taps, filter_taps, skip_bias, out_weight):
    tables = [jnp.asarray(t) for t in fourier_tables()]
    near = pl.BlockSpec(memory_space=pltpu.VMEM)
    far = pl.BlockSpec(memory_space=pl.ANY)
    dma, vmem = pltpu.SemaphoreType.DMA, pltpu.VMEM
    return pl.pallas_call(
        kernel,
        out_shape=jax.ShapeDtypeStruct((ROWS, CHAN), bf16),
        in_specs=[far] * 4 + [near] * 7,
        out_specs=near,
        scratch_shapes=[
            vmem((3, ROWS, CHAN), bf16),
            vmem((ROWS, CHAN), f32),
            vmem((4, 2 * ROWS, 2 * ROWS), bf16),
            vmem((3, 16, CHAN), bf16),
            *[vmem((2, CHAN, 128), bf16)] * 6,
            vmem((2, CHAN, 128), f32),
            vmem((SHARE // GROUP, GROUP * BLOCKS, 2 * ROWS), f32),
            vmem((ROWS, CHAN), f32),
            vmem((ROWS, CHAN), f32),
            vmem((4, 8, 2, 64, CHAN), bf16),
            vmem((4, 2, ROWS, WAVE), bf16),
            vmem((ROWS, CHAN), f32),
            dma((3,)),
            pltpu.SemaphoreType.REGULAR((2,)),
            dma((2,)),
            *[dma((2, 2))] * 3,
            dma((2,)),
            *[dma((2, 4))] * 2,
            *[dma((2, 8))] * 2,
            *[dma((8,))] * 2,
            *[dma((4, 8))] * 2,
            *[dma((2, 4))] * 2,
        ],
        compiler_params=pltpu.CompilerParams(
            collective_id=0, has_side_effects=True, vmem_limit_bytes=60 * 1024 * 1024
        ),
    )(
        features, filter_taps, out_weight.T, tables[5],
        short_taps, skip_bias[None, :], *tables[:5],
    )


def solution(mesh):
    placed = (P(None, "seq", "ch"), P(None, None, "ch"), P("seq", "ch"), P("ch"), P("ch", "seq"))
    return jax.shard_map(
        shards, mesh=mesh, in_specs=placed, out_specs=P("seq", "ch"), check_vma=False
    )
```

```python
import functools
import math

import jax
import jax.numpy as jnp
import numpy as np
from jax import lax
from jax.experimental import pallas as pl
from jax.experimental.pallas import tpu as pltpu
from jax.sharding import PartitionSpec as P

MESH = pl.DeviceIdType.MESH
f32, bf16 = jnp.float32, jnp.bfloat16

BLOCKS = 64
ROWS = 256
CHAN = 1024
SHARE = CHAN // BLOCKS
POINTS = 2 * BLOCKS * ROWS
GROUP = 4
WAVE = CHAN // 2


def split_np(table):
    high = np.asarray(table, np.float32).astype(jnp.bfloat16)
    low = (np.asarray(table, np.float64) - high.astype(np.float64)).astype(jnp.bfloat16)
    return high, low


@functools.lru_cache(maxsize=None)
def fourier_tables():
    steps = np.arange(BLOCKS) + 0.5
    outer = 2 * np.pi * np.outer(steps, np.arange(BLOCKS)) / (2 * BLOCKS)
    block_forward = np.concatenate([np.cos(outer), -np.sin(outer)], axis=0)
    block_inverse = block_forward.T * (2.0 / POINTS)
    twist = 2 * np.pi * np.outer(steps, np.arange(ROWS)) / POINTS
    inner = 2 * np.pi * (np.outer(np.arange(ROWS), np.arange(ROWS)) % ROWS) / ROWS
    cos_in, sin_in = np.cos(inner), np.sin(inner)
    row_forward = np.block([[cos_in, -sin_in], [sin_in, cos_in]])
    row_inverse = np.block([[cos_in, sin_in], [-sin_in, cos_in]])
    return (
        np.concatenate(split_np(block_forward), axis=1),
        *split_np(block_inverse),
        np.cos(twist).astype(np.float32),
        np.sin(twist).astype(np.float32),
        np.stack(split_np(row_forward) + split_np(row_inverse)),
    )


def split(value):
    high = value.astype(bf16)
    return high, (value - high.astype(f32)).astype(bf16)


def dot(left, right):
    return jnp.dot(left, right, preferred_element_type=f32)


def dot_wide(left, right_high, right_low):
    high, low = split(left)
    return dot(high, right_high) + (dot(high, right_low) + dot(low, right_high))


def kernel(
    feat_far, filt_far, weight_far, row_far, taps, skip, bf, bi_hi, bi_lo, tw_cos, tw_sin,
    out,
    feat, filt, rows, halo, f_out, g_out, f_in, g_in, y_out, y_in,
    wide, spec, query, gated, w_all, hyena, acc,
    load_sems, greet_sems, halo_sems, f_sems, g_sems, y_sems, t_sems,
    z_send, z_recv, v_send, v_recv, u_send, u_recv, p_send, p_recv, h_send, h_recv,
):
    me = lax.axis_index("seq")
    col = lax.axis_index("ch")
    row = lax.div(me, 16)
    deep = lax.div(lax.rem(me, 16), 2)
    core = lax.rem(me, 2)

    def seq_at(r, d, c):
        return (r * 8 + d) * 2 + c

    def wrap(i, n):
        return lax.rem(i + n, n)

    def signal(sem, **where):
        pl.semaphore_signal(sem, inc=1, device_id=where, device_id_type=MESH)

    def remote(src, dst, send, recv, **where):
        return pltpu.make_async_remote_copy(
            src_ref=src, dst_ref=dst, send_sem=send, recv_sem=recv, device_id=where, device_id_type=MESH
        )

    barrier = pltpu.get_barrier_semaphore()
    after_me, before_me = lax.rem(me + 1, BLOCKS), wrap(me - 1, BLOCKS)
    mirror = {"seq": seq_at(col, deep, core), "ch": row}
    signal(barrier, seq=seq_at(row, deep, 1 - core))
    signal(barrier, seq=jnp.where(core == 0, before_me, after_me))
    for step in range(1, 8):
        signal(barrier, seq=seq_at(row, lax.rem(deep + step, 8), core))
    for step in range(1, 4):
        signal(barrier, seq=seq_at(lax.rem(row + step, 4), deep, core))
    for step in (1, 3):
        signal(barrier, ch=lax.rem(col + step, 4))

    @pl.when(row != col)
    def _():
        signal(barrier, **mirror)

    loads = [
        pltpu.make_async_copy(far, near, load_sems.at[i])
        for i, (far, near) in enumerate(((filt_far, filt), (feat_far, feat), (row_far, rows)))
    ]
    for load in loads:
        load.start()
    loads[0].wait()

    def packed(value, wave):
        turned = value[:, wave * WAVE : (wave + 1) * WAVE].T
        parts = [turned[:, h * 128 : (h + 1) * 128].reshape(BLOCKS, 8, 128) for h in range(2)]
        return jnp.concatenate(parts, axis=1).reshape(CHAN, 128).astype(bf16)

    f_out[0] = packed(filt[...], 0)

    pl.semaphore_wait(barrier, 14 + (row != col).astype(jnp.int32))

    halo_copy = remote(
        feat_far.at[:, pl.ds(ROWS - 16, 16), :], halo, halo_sems.at[0], halo_sems.at[1], seq=after_me
    )
    halo_copy.start()

    mirror_copy = remote(weight_far, w_all.at[col, deep, core], t_sems.at[0], t_sems.at[1], **mirror)
    same_copy = pltpu.make_async_copy(weight_far, w_all.at[row, deep, core], t_sems.at[1])

    @pl.when(row != col)
    def _():
        mirror_copy.start()

    @pl.when(row == col)
    def _():
        same_copy.start()

    def share_to(src, dst, sems, to):
        remote(
            src.at[pl.ds(pl.multiple_of(to * SHARE, SHARE), SHARE)],
            dst.at[pl.ds(pl.multiple_of(me * SHARE, SHARE), SHARE)],
            sems.at[0], sems.at[1], seq=to,
        ).start()

    def exchange(src, dst, sems, begin=1, end=BLOCKS):
        def send(k, carry):
            share_to(src, dst, sems, lax.rem(me + k * STRIDE, BLOCKS))
            return carry

        lax.fori_loop(begin, end, send, 0)
        if begin == 1:
            here = pl.ds(pl.multiple_of(me * SHARE, SHARE), SHARE)
            dst[here, :] = src[here, :]

    for step in range(1, 4):
        signal(greet_sems.at[0], seq=seq_at(lax.rem(row + step, 4), deep, core))

    def to_line(k, carry):
        share_to(f_out.at[0], f_in.at[0], f_sems.at[0], seq_at(row, lax.rem(deep + 3 * k, 8), core))
        return carry

    def to_core(k, carry):
        near_by = seq_at(lax.rem(row + 1 + lax.rem(k, 3), 4), lax.rem(deep + 3 * k, 8), core)
        share_to(f_out.at[0], f_in.at[0], f_sems.at[0], near_by)
        return carry

    def to_other(k, carry):
        at = row * 8 + deep + 11 * k
        share_to(f_out.at[0], f_in.at[0], f_sems.at[0], lax.rem(at, 32) * 2 + 1 - core)
        return carry

    lax.fori_loop(1, 8, to_line, 0)
    here = pl.ds(pl.multiple_of(me * SHARE, SHARE), SHARE)
    f_in[0, here, :] = f_out[0, here, :]
    loads[1].wait()
    first = (me != 0).astype(f32)

    def mixed(b):
        middle = feat[b].astype(f32)
        back_one = pltpu.roll(middle, 1, 0)
        back_two = pltpu.roll(middle, 2, 0)
        return taps[b, 0:1] * middle + taps[b, 1:2] * back_one + taps[b, 2:3] * back_two

    def mixed_top(b):
        top = feat[b, 0:16].astype(f32)
        joined = jnp.concatenate([halo[b].astype(f32) * first, top], axis=0)
        back_one = pltpu.roll(joined, 1, 0)[16:]
        back_two = pltpu.roll(joined, 2, 0)[16:]
        return taps[b, 0:1] * top + taps[b, 1:2] * back_one + taps[b, 2:3] * back_two

    pl.semaphore_wait(greet_sems.at[0], 3)
    signal(greet_sems.at[1], seq=seq_at(row, deep, 1 - core))
    lax.fori_loop(0, 24, to_core, 0)
    pl.semaphore_wait(greet_sems.at[1], 1)
    gated[...] = mixed(1) * mixed(2)

    def exchanged(src, dst, sems):
        others = pl.ds(0, (BLOCKS - 1) * SHARE)
        pltpu.make_async_copy(src.at[others], dst.at[others], sems.at[1]).wait()
        pltpu.make_async_copy(src.at[others], dst.at[others], sems.at[0]).wait()

    def z_copies(i):
        parts = (pl.ds(0, 64), pl.ds(0, 64)) if i < 3 else (pl.ds(0, 32), pl.ds(32, 32))
        up = w_all.at[row, wrap(deep - i, 8), core, parts[0]]
        down = w_all.at[row, lax.rem(deep + i, 8), core, parts[1]]
        return (
            remote(up, up, z_send.at[0, i], z_recv.at[0, i], seq=seq_at(row, lax.rem(deep + 1, 8), core)),
            remote(down, down, z_send.at[1, i], z_recv.at[1, i], seq=seq_at(row, lax.rem(deep + 7, 8), core)),
        )

    up_row, down_row = lax.rem(row + 1, 4), wrap(row - 1, 4)

    def v_copies(i):
        block = w_all.at[row, lax.rem(deep + i, 8), core]
        return (
            remote(block, block, v_send.at[0, i], v_recv.at[0, i], seq=seq_at(up_row, deep, core)),
            remote(block, block, v_send.at[1, i], v_recv.at[1, i], seq=seq_at(down_row, deep, core)),
        )

    def u_copy(i):
        source, to = (down_row, up_row) if i < 4 else (up_row, down_row)
        block = w_all.at[source, lax.rem(deep + i, 8), core]
        return remote(block, block, u_send.at[i], u_recv.at[i], seq=seq_at(to, deep, core))

    z_steps = [z_copies(i) for i in range(4)]
    v_steps = [v_copies(i) for i in range(8)]
    u_steps = [u_copy(i) for i in range(8)]

    def start(copies):
        for copy in copies:
            copy.start()

    def received(copies):
        for copy in copies:
            copy.wait_recv()

    def p_copy(i, slot):
        ref = w_all.at[lax.rem(row + i, 4), lax.rem(deep + slot, 8), core]
        return remote(ref, ref, p_send.at[i, slot], p_recv.at[i, slot], seq=seq_at(row, deep, 1 - core))

    p_copies = [[p_copy(i, slot) for slot in range(8)] for i in range(4)]

    def spread(slot):
        start(v_steps[slot])
        p_copies[0][slot].start()

    def take_lines(slot):
        v_steps[slot][0].wait_recv()
        if slot < 4:
            u_steps[slot].start()
        p_copies[3][slot].start()
        v_steps[slot][1].wait_recv()
        if slot >= 4:
            u_steps[slot].start()
        p_copies[1][slot].start()

    lax.fori_loop(0, 32, to_other, 0)
    f_out[1] = packed(filt[...], 1)

    halo_copy.wait()
    gated[0:16] = mixed_top(1) * mixed_top(2)
    for wave in range(2):
        g_out[wave] = packed(gated[...], wave)

    def share(src, dst, sems, wave, begin=1, end=BLOCKS):
        exchange(src.at[wave], dst.at[wave], sems.at[wave], begin, end)

    share(g_out, g_in, g_sems, 0)

    @pl.when(row != col)
    def _():
        mirror_copy.wait()

    @pl.when(row == col)
    def _():
        same_copy.wait()

    start(z_steps[0])
    spread(0)
    share(f_out, f_in, f_sems, 1)
    query[...] = mixed(0)
    query[0:16] = mixed_top(0)
    received(z_steps[0])
    start(z_steps[1])
    spread(1)
    spread(7)
    share(g_out, g_in, g_sems, 1)

    def spectra(wave, q):
        lines = []
        for c in range(GROUP):
            line = jnp.concatenate([wide[wave, every, :] for every in every_block(q, c)], axis=1)
            both = dot(bf[...], jnp.concatenate([line, line], axis=0).astype(bf16))
            real, imag = both[:BLOCKS], both[BLOCKS:]
            lines.append(
                jnp.concatenate(
                    [
                        real * tw_cos[...] + imag * tw_sin[...],
                        imag * tw_cos[...] - real * tw_sin[...],
                    ],
                    axis=1,
                )
            )
        return dot_wide(jnp.concatenate(lines, axis=0), rows[0], rows[1])

    def every_block(q, c):
        return [pl.ds(q * GROUP + c + 8 * h, BLOCKS, stride=SHARE) for h in range(2)]

    def filter_wave(wave):
        exchanged(f_out.at[wave], f_in.at[wave], f_sems.at[wave])
        wide[wave] = f_in[wave].astype(f32)

        def filter_group(q, carry):
            spec[2 * wave + q] = spectra(wave, q)
            return carry

        lax.fori_loop(0, 2, filter_group, 0)

    def conv_wave(wave):
        exchanged(g_out.at[wave], g_in.at[wave], g_sems.at[wave])
        wide[wave] = g_in[wave].astype(f32)

        def conv_group(q, carry):
            spectrum = spectra(wave, q)
            taps_spec = spec[2 * wave + q]
            sr, si = spectrum[:, :ROWS], spectrum[:, ROWS:]
            tr, ti = taps_spec[:, :ROWS], taps_spec[:, ROWS:]
            joint = jnp.concatenate([sr * tr - si * ti, sr * ti + si * tr], axis=1)
            back = dot_wide(joint, rows[2], rows[3])
            for c in range(GROUP):
                real = back[c * BLOCKS : (c + 1) * BLOCKS, :ROWS]
                imag = back[c * BLOCKS : (c + 1) * BLOCKS, ROWS:]
                both = jnp.concatenate(
                    [
                        real * tw_cos[...] - imag * tw_sin[...],
                        imag * tw_cos[...] + real * tw_sin[...],
                    ],
                    axis=0,
                )
                high, low = split(both)
                series = dot(bi_hi[...], high) + (dot(bi_hi[...], low) + dot(bi_lo[...], high))
                for h, every in enumerate(every_block(q, c)):
                    wide[wave, every, :] = series[:, h * 128 : (h + 1) * 128]
            return carry

        lax.fori_loop(0, 2, conv_group, 0)
        y_out[wave] = wide[wave].astype(bf16)
        share(y_out, y_in, y_sems, wave)

    loads[2].wait()
    filter_wave(0)
    received(z_steps[1])
    start(z_steps[2])
    spread(2)
    spread(6)
    conv_wave(0)
    received(z_steps[2])
    start(z_steps[3])
    spread(3)
    spread(5)
    take_lines(0)
    filter_wave(1)
    received(z_steps[3])
    spread(4)
    for slot in EARLY:
        take_lines(slot)
    conv_wave(1)
    for slot in MIDDLE:
        take_lines(slot)

    left, right = wrap(col - 1, 4), lax.rem(col + 1, 4)

    def h_copies(wave, step):
        first_half, second_half = pl.ds(0, 128), pl.ds(128, 128)
        if step == 0:
            up, down = hyena.at[col, wave, first_half], hyena.at[col, wave, second_half]
        elif step == 1:
            up, down = hyena.at[col, wave, second_half], hyena.at[col, wave, first_half]
        else:
            up, down = hyena.at[left, wave, first_half], hyena.at[right, wave, second_half]
        i = 2 * step + wave
        return (
            remote(up, up, h_send.at[0, i], h_recv.at[0, i], ch=right),
            remote(down, down, h_send.at[1, i], h_recv.at[1, i], ch=left),
        )

    h_own = [h_copies(wave, 0) for wave in range(2)]
    h_rest = [h_copies(wave, 1) for wave in range(2)]
    h_far = [h_copies(wave, 2) for wave in range(2)]

    def finish(wave):
        exchanged(y_out.at[wave], y_in.at[wave], y_sems.at[wave])
        series = y_in[wave].astype(f32).reshape(BLOCKS, SHARE, 128)
        lanes = slice(wave * WAVE, (wave + 1) * WAVE)
        for h in range(2):
            part = slice(h * 128, h * 128 + 128)
            long_conv = series[:, 8 * h : 8 * h + 8].reshape(WAVE, 128).T
            hyena[col, wave, part] = (
                query[part, lanes] * (long_conv + skip[:, lanes] * gated[part, lanes])
            ).astype(bf16)
        start(h_own[wave])
        start(h_rest[wave])

    def project(source, wave, fresh=False):
        def tile(j, carry):
            cols = pl.ds(pl.multiple_of(j * 256, 256), 256)
            block = w_all[source, pl.ds(2 * j, 2), :, :, wave * WAVE : (wave + 1) * WAVE]
            sums = lax.dot_general(
                hyena[source, wave], block.reshape(256, WAVE), (((1,), (1,)), ((), ())),
                preferred_element_type=f32,
            )
            acc[:, cols] = sums if fresh else acc[:, cols] + sums
            return carry

        lax.fori_loop(0, 4, tile, 0)

    finish(0)
    for slot in LATE[:-1]:
        take_lines(slot)
    received(h_own[0])
    start(h_far[0])
    finish(1)
    for slot in LATE[-1:]:
        take_lines(slot)
    for slot in range(8):
        u_steps[slot].wait_recv()
        p_copies[2][slot].start()
    for copies in p_copies:
        received(copies)
    project(col, 0, True)
    received(h_own[1])
    start(h_far[1])
    received(h_rest[0])
    project(left, 0)
    project(right, 0)
    project(col, 1)
    received(h_far[0])
    project(lax.rem(col + 2, 4), 0)
    received(h_rest[1])
    project(left, 1)
    project(right, 1)
    received(h_far[1])
    project(lax.rem(col + 2, 4), 1)
    out[...] = acc[...].astype(bf16)

    for copies in (*z_steps, *v_steps, u_steps, *p_copies, *h_own, *h_rest, *h_far):
        for copy in copies:
            copy.wait_send()


STRIDE = 23
EARLY, MIDDLE, LATE = (1, 7), (2, 6), (3, 5, 4)


def shards(features, short_taps, filter_taps, skip_bias, out_weight):
    tables = [jnp.asarray(t) for t in fourier_tables()]
    near = pl.BlockSpec(memory_space=pltpu.VMEM)
    far = pl.BlockSpec(memory_space=pl.ANY)
    dma, vmem = pltpu.SemaphoreType.DMA, pltpu.VMEM
    return pl.pallas_call(
        kernel,
        out_shape=jax.ShapeDtypeStruct((ROWS, CHAN), bf16),
        in_specs=[far] * 4 + [near] * 7,
        out_specs=near,
        scratch_shapes=[
            vmem((3, ROWS, CHAN), bf16),
            vmem((ROWS, CHAN), f32),
            vmem((4, 2 * ROWS, 2 * ROWS), bf16),
            vmem((3, 16, CHAN), bf16),
            *[vmem((2, CHAN, 128), bf16)] * 6,
            vmem((2, CHAN, 128), f32),
            vmem((SHARE // GROUP, GROUP * BLOCKS, 2 * ROWS), f32),
            vmem((ROWS, CHAN), f32),
            vmem((ROWS, CHAN), f32),
            vmem((4, 8, 2, 64, CHAN), bf16),
            vmem((4, 2, ROWS, WAVE), bf16),
            vmem((ROWS, CHAN), f32),
            dma((3,)),
            pltpu.SemaphoreType.REGULAR((2,)),
            dma((2,)),
            *[dma((2, 2))] * 3,
            dma((2,)),
            *[dma((2, 4))] * 2,
            *[dma((2, 8))] * 2,
            *[dma((8,))] * 2,
            *[dma((4, 8))] * 2,
            *[dma((2, 6))] * 2,
        ],
        compiler_params=pltpu.CompilerParams(
            collective_id=0, has_side_effects=True, vmem_limit_bytes=60 * 1024 * 1024
        ),
    )(
        features, filter_taps, out_weight.T, tables[5],
        short_taps, skip_bias[None, :], *tables[:5],
    )


def solution(mesh):
    placed = (P(None, "seq", "ch"), P(None, None, "ch"), P("seq", "ch"), P("ch"), P("ch", "seq"))
    return jax.shard_map(
        shards, mesh=mesh, in_specs=placed, out_specs=P("seq", "ch"), check_vma=False
    )
```

```python
import functools
import math

import jax
import jax.numpy as jnp
import numpy as np
from jax import lax
from jax.experimental import pallas as pl
from jax.experimental.pallas import tpu as pltpu
from jax.sharding import PartitionSpec as P

MESH = pl.DeviceIdType.MESH
f32, bf16 = jnp.float32, jnp.bfloat16

BLOCKS = 64
ROWS = 256
CHAN = 1024
SHARE = CHAN // BLOCKS
POINTS = 2 * BLOCKS * ROWS
GROUP = 4
WAVE = CHAN // 2


def split_np(table):
    high = np.asarray(table, np.float32).astype(jnp.bfloat16)
    low = (np.asarray(table, np.float64) - high.astype(np.float64)).astype(jnp.bfloat16)
    return high, low


@functools.lru_cache(maxsize=None)
def fourier_tables():
    steps = np.arange(BLOCKS) + 0.5
    outer = 2 * np.pi * np.outer(steps, np.arange(BLOCKS)) / (2 * BLOCKS)
    block_forward = np.concatenate([np.cos(outer), -np.sin(outer)], axis=0)
    block_inverse = block_forward.T * (2.0 / POINTS)
    twist = 2 * np.pi * np.outer(steps, np.arange(ROWS)) / POINTS
    inner = 2 * np.pi * (np.outer(np.arange(ROWS), np.arange(ROWS)) % ROWS) / ROWS
    cos_in, sin_in = np.cos(inner), np.sin(inner)
    row_forward = np.block([[cos_in, -sin_in], [sin_in, cos_in]])
    row_inverse = np.block([[cos_in, sin_in], [-sin_in, cos_in]])
    return (
        np.concatenate(split_np(block_forward), axis=1),
        *split_np(block_inverse),
        np.cos(twist).astype(np.float32),
        np.sin(twist).astype(np.float32),
        np.stack(split_np(row_forward) + split_np(row_inverse)),
    )


def split(value):
    high = value.astype(bf16)
    return high, (value - high.astype(f32)).astype(bf16)


def dot(left, right):
    return jnp.dot(left, right, preferred_element_type=f32)


def dot_wide(left, right_high, right_low):
    high, low = split(left)
    return dot(high, right_high) + (dot(high, right_low) + dot(low, right_high))


def kernel(
    feat_far, filt_far, weight_far, row_far, taps, skip, bf, bi_hi, bi_lo, tw_cos, tw_sin,
    out,
    feat, filt, rows, halo, f_out, g_out, f_in, g_in, y_out, y_in,
    wide, spec, query, gated, w_all, hyena, acc,
    load_sems, greet_sems, halo_sems, f_sems, g_sems, y_sems, t_sems,
    z_send, z_recv, v_send, v_recv, u_send, u_recv, p_send, p_recv, h_send, h_recv,
):
    me = lax.axis_index("seq")
    col = lax.axis_index("ch")
    row = lax.div(me, 16)
    deep = lax.div(lax.rem(me, 16), 2)
    core = lax.rem(me, 2)

    def seq_at(r, d, c):
        return (r * 8 + d) * 2 + c

    def wrap(i, n):
        return lax.rem(i + n, n)

    def signal(sem, **where):
        pl.semaphore_signal(sem, inc=1, device_id=where, device_id_type=MESH)

    def remote(src, dst, send, recv, **where):
        return pltpu.make_async_remote_copy(
            src_ref=src, dst_ref=dst, send_sem=send, recv_sem=recv, device_id=where, device_id_type=MESH
        )

    barrier = pltpu.get_barrier_semaphore()
    after_me, before_me = lax.rem(me + 1, BLOCKS), wrap(me - 1, BLOCKS)
    mirror = {"seq": seq_at(col, deep, core), "ch": row}
    signal(barrier, seq=seq_at(row, deep, 1 - core))
    signal(barrier, seq=jnp.where(core == 0, before_me, after_me))
    for step in range(1, 8):
        signal(barrier, seq=seq_at(row, lax.rem(deep + step, 8), core))
    for step in range(1, 4):
        signal(barrier, seq=seq_at(lax.rem(row + step, 4), deep, core))
    for step in (1, 3):
        signal(barrier, ch=lax.rem(col + step, 4))

    @pl.when(row != col)
    def _():
        signal(barrier, **mirror)

    loads = [
        pltpu.make_async_copy(far, near, load_sems.at[i])
        for i, (far, near) in enumerate(((filt_far, filt), (feat_far, feat), (row_far, rows)))
    ]
    for load in loads:
        load.start()
    loads[0].wait()

    def packed(value, wave):
        turned = value[:, wave * WAVE : (wave + 1) * WAVE].T
        parts = [turned[:, h * 128 : (h + 1) * 128].reshape(BLOCKS, 8, 128) for h in range(2)]
        return jnp.concatenate(parts, axis=1).reshape(CHAN, 128).astype(bf16)

    f_out[0] = packed(filt[...], 0)

    pl.semaphore_wait(barrier, 14 + (row != col).astype(jnp.int32))

    halo_copy = remote(
        feat_far.at[:, pl.ds(ROWS - 16, 16), :], halo, halo_sems.at[0], halo_sems.at[1], seq=after_me
    )
    halo_copy.start()

    mirror_copy = remote(weight_far, w_all.at[col, deep, core], t_sems.at[0], t_sems.at[1], **mirror)
    same_copy = pltpu.make_async_copy(weight_far, w_all.at[row, deep, core], t_sems.at[1])

    @pl.when(row != col)
    def _():
        mirror_copy.start()

    @pl.when(row == col)
    def _():
        same_copy.start()

    def share_to(src, dst, sems, to):
        remote(
            src.at[pl.ds(pl.multiple_of(to * SHARE, SHARE), SHARE)],
            dst.at[pl.ds(pl.multiple_of(me * SHARE, SHARE), SHARE)],
            sems.at[0], sems.at[1], seq=to,
        ).start()

    def exchange(src, dst, sems, begin=1, end=BLOCKS):
        def send(k, carry):
            share_to(src, dst, sems, lax.rem(me + k * STRIDE, BLOCKS))
            return carry

        lax.fori_loop(begin, end, send, 0)
        if begin == 1:
            here = pl.ds(pl.multiple_of(me * SHARE, SHARE), SHARE)
            dst[here, :] = src[here, :]

    for step in range(1, 4):
        signal(greet_sems.at[0], seq=seq_at(lax.rem(row + step, 4), deep, core))

    def to_line(k, carry):
        share_to(f_out.at[0], f_in.at[0], f_sems.at[0], seq_at(row, lax.rem(deep + 3 * k, 8), core))
        return carry

    def to_core(k, carry):
        near_by = seq_at(lax.rem(row + 1 + lax.rem(k, 3), 4), lax.rem(deep + 3 * k, 8), core)
        share_to(f_out.at[0], f_in.at[0], f_sems.at[0], near_by)
        return carry

    def to_other(k, carry):
        at = row * 8 + deep + 11 * k
        share_to(f_out.at[0], f_in.at[0], f_sems.at[0], lax.rem(at, 32) * 2 + 1 - core)
        return carry

    lax.fori_loop(1, 8, to_line, 0)
    here = pl.ds(pl.multiple_of(me * SHARE, SHARE), SHARE)
    f_in[0, here, :] = f_out[0, here, :]
    loads[1].wait()
    first = (me != 0).astype(f32)

    def mixed(b):
        middle = feat[b].astype(f32)
        back_one = pltpu.roll(middle, 1, 0)
        back_two = pltpu.roll(middle, 2, 0)
        return taps[b, 0:1] * middle + taps[b, 1:2] * back_one + taps[b, 2:3] * back_two

    def mixed_top(b):
        top = feat[b, 0:16].astype(f32)
        joined = jnp.concatenate([halo[b].astype(f32) * first, top], axis=0)
        back_one = pltpu.roll(joined, 1, 0)[16:]
        back_two = pltpu.roll(joined, 2, 0)[16:]
        return taps[b, 0:1] * top + taps[b, 1:2] * back_one + taps[b, 2:3] * back_two

    pl.semaphore_wait(greet_sems.at[0], 3)
    signal(greet_sems.at[1], seq=seq_at(row, deep, 1 - core))
    lax.fori_loop(0, 24, to_core, 0)
    pl.semaphore_wait(greet_sems.at[1], 1)
    gated[...] = mixed(1) * mixed(2)

    def exchanged(src, dst, sems):
        others = pl.ds(0, (BLOCKS - 1) * SHARE)
        pltpu.make_async_copy(src.at[others], dst.at[others], sems.at[1]).wait()
        pltpu.make_async_copy(src.at[others], dst.at[others], sems.at[0]).wait()

    def z_copies(i):
        parts = (pl.ds(0, 64), pl.ds(0, 64)) if i < 3 else (pl.ds(0, 32), pl.ds(32, 32))
        up = w_all.at[row, wrap(deep - i, 8), core, parts[0]]
        down = w_all.at[row, lax.rem(deep + i, 8), core, parts[1]]
        return (
            remote(up, up, z_send.at[0, i], z_recv.at[0, i], seq=seq_at(row, lax.rem(deep + 1, 8), core)),
            remote(down, down, z_send.at[1, i], z_recv.at[1, i], seq=seq_at(row, lax.rem(deep + 7, 8), core)),
        )

    up_row, down_row = lax.rem(row + 1, 4), wrap(row - 1, 4)

    def v_copies(i):
        block = w_all.at[row, lax.rem(deep + i, 8), core]
        return (
            remote(block, block, v_send.at[0, i], v_recv.at[0, i], seq=seq_at(up_row, deep, core)),
            remote(block, block, v_send.at[1, i], v_recv.at[1, i], seq=seq_at(down_row, deep, core)),
        )

    def u_copy(i):
        source, to = (down_row, up_row) if i < 4 else (up_row, down_row)
        block = w_all.at[source, lax.rem(deep + i, 8), core]
        return remote(block, block, u_send.at[i], u_recv.at[i], seq=seq_at(to, deep, core))

    z_steps = [z_copies(i) for i in range(4)]
    v_steps = [v_copies(i) for i in range(8)]
    u_steps = [u_copy(i) for i in range(8)]

    def start(copies):
        for copy in copies:
            copy.start()

    def received(copies):
        for copy in copies:
            copy.wait_recv()

    def p_copy(i, slot):
        ref = w_all.at[lax.rem(row + i, 4), lax.rem(deep + slot, 8), core]
        return remote(ref, ref, p_send.at[i, slot], p_recv.at[i, slot], seq=seq_at(row, deep, 1 - core))

    p_copies = [[p_copy(i, slot) for slot in range(8)] for i in range(4)]

    def spread(slot):
        start(v_steps[slot])
        p_copies[0][slot].start()

    def take_lines(slot):
        v_steps[slot][0].wait_recv()
        if slot < 4:
            u_steps[slot].start()
        p_copies[3][slot].start()
        v_steps[slot][1].wait_recv()
        if slot >= 4:
            u_steps[slot].start()
        p_copies[1][slot].start()

    lax.fori_loop(0, 32, to_other, 0)
    f_out[1] = packed(filt[...], 1)

    halo_copy.wait()
    gated[0:16] = mixed_top(1) * mixed_top(2)
    for wave in range(2):
        g_out[wave] = packed(gated[...], wave)

    def share(src, dst, sems, wave, begin=1, end=BLOCKS):
        exchange(src.at[wave], dst.at[wave], sems.at[wave], begin, end)

    share(g_out, g_in, g_sems, 0)

    @pl.when(row != col)
    def _():
        mirror_copy.wait()

    @pl.when(row == col)
    def _():
        same_copy.wait()

    start(z_steps[0])
    spread(0)
    share(f_out, f_in, f_sems, 1)
    query[...] = mixed(0)
    query[0:16] = mixed_top(0)
    received(z_steps[0])
    start(z_steps[1])
    spread(1)
    spread(7)
    share(g_out, g_in, g_sems, 1)

    def spectra(wave, q):
        lines = []
        for c in range(GROUP):
            line = jnp.concatenate([wide[wave, every, :] for every in every_block(q, c)], axis=1)
            both = dot(bf[...], jnp.concatenate([line, line], axis=0).astype(bf16))
            real, imag = both[:BLOCKS], both[BLOCKS:]
            lines.append(
                jnp.concatenate(
                    [
                        real * tw_cos[...] + imag * tw_sin[...],
                        imag * tw_cos[...] - real * tw_sin[...],
                    ],
                    axis=1,
                )
            )
        return dot_wide(jnp.concatenate(lines, axis=0), rows[0], rows[1])

    def every_block(q, c):
        return [pl.ds(q * GROUP + c + 8 * h, BLOCKS, stride=SHARE) for h in range(2)]

    def filter_wave(wave):
        exchanged(f_out.at[wave], f_in.at[wave], f_sems.at[wave])
        wide[wave] = f_in[wave].astype(f32)

        def filter_group(q, carry):
            spec[2 * wave + q] = spectra(wave, q)
            return carry

        lax.fori_loop(0, 2, filter_group, 0)

    def conv_wave(wave):
        exchanged(g_out.at[wave], g_in.at[wave], g_sems.at[wave])
        wide[wave] = g_in[wave].astype(f32)

        def conv_group(q, carry):
            spectrum = spectra(wave, q)
            taps_spec = spec[2 * wave + q]
            sr, si = spectrum[:, :ROWS], spectrum[:, ROWS:]
            tr, ti = taps_spec[:, :ROWS], taps_spec[:, ROWS:]
            joint = jnp.concatenate([sr * tr - si * ti, sr * ti + si * tr], axis=1)
            back = dot_wide(joint, rows[2], rows[3])
            for c in range(GROUP):
                real = back[c * BLOCKS : (c + 1) * BLOCKS, :ROWS]
                imag = back[c * BLOCKS : (c + 1) * BLOCKS, ROWS:]
                both = jnp.concatenate(
                    [
                        real * tw_cos[...] - imag * tw_sin[...],
                        imag * tw_cos[...] + real * tw_sin[...],
                    ],
                    axis=0,
                )
                high, low = split(both)
                series = dot(bi_hi[...], high) + (dot(bi_hi[...], low) + dot(bi_lo[...], high))
                for h, every in enumerate(every_block(q, c)):
                    wide[wave, every, :] = series[:, h * 128 : (h + 1) * 128]
            return carry

        lax.fori_loop(0, 2, conv_group, 0)
        y_out[wave] = wide[wave].astype(bf16)
        share(y_out, y_in, y_sems, wave)

    loads[2].wait()
    filter_wave(0)
    received(z_steps[1])
    start(z_steps[2])
    spread(2)
    spread(6)
    conv_wave(0)
    received(z_steps[2])
    start(z_steps[3])
    spread(3)
    spread(5)
    take_lines(0)
    filter_wave(1)
    received(z_steps[3])
    spread(4)
    for slot in EARLY:
        take_lines(slot)
    conv_wave(1)
    for slot in MIDDLE:
        take_lines(slot)

    left, right = wrap(col - 1, 4), lax.rem(col + 1, 4)

    def h_copies(wave, step):
        first_half, second_half = pl.ds(0, 128), pl.ds(128, 128)
        if step == 0:
            up, down = hyena.at[col, wave, first_half], hyena.at[col, wave, second_half]
        elif step == 1:
            up, down = hyena.at[col, wave, second_half], hyena.at[col, wave, first_half]
        else:
            up, down = hyena.at[left, wave, first_half], hyena.at[right, wave, second_half]
        i = 2 * step + wave
        return (
            remote(up, up, h_send.at[0, i], h_recv.at[0, i], ch=right),
            remote(down, down, h_send.at[1, i], h_recv.at[1, i], ch=left),
        )

    h_own = [h_copies(wave, 0) for wave in range(2)]
    h_rest = [h_copies(wave, 1) for wave in range(2)]
    h_far = [h_copies(wave, 2) for wave in range(2)]

    def finish(wave):
        exchanged(y_out.at[wave], y_in.at[wave], y_sems.at[wave])
        series = y_in[wave].astype(f32).reshape(BLOCKS, SHARE, 128)
        lanes = slice(wave * WAVE, (wave + 1) * WAVE)
        for h in range(2):
            part = slice(h * 128, h * 128 + 128)
            long_conv = series[:, 8 * h : 8 * h + 8].reshape(WAVE, 128).T
            hyena[col, wave, part] = (
                query[part, lanes] * (long_conv + skip[:, lanes] * gated[part, lanes])
            ).astype(bf16)
        start(h_own[wave])
        start(h_rest[wave])

    def project(source, wave, fresh=False):
        def tile(j, carry):
            cols = pl.ds(pl.multiple_of(j * 256, 256), 256)
            block = w_all[source, pl.ds(2 * j, 2), :, :, wave * WAVE : (wave + 1) * WAVE]
            sums = lax.dot_general(
                hyena[source, wave], block.reshape(256, WAVE), (((1,), (1,)), ((), ())),
                preferred_element_type=f32,
            )
            acc[:, cols] = sums if fresh else acc[:, cols] + sums
            return carry

        lax.fori_loop(0, 4, tile, 0)

    finish(0)
    for slot in LATE[:-1]:
        take_lines(slot)
    received(h_own[0])
    start(h_far[0])
    finish(1)
    for slot in LATE[-1:]:
        take_lines(slot)
    for slot in range(8):
        u_steps[slot].wait_recv()
        p_copies[2][slot].start()
    received(h_own[1])
    start(h_far[1])
    for copies in p_copies:
        received(copies)
    project(col, 0, True)
    received(h_rest[0])
    project(left, 0)
    project(right, 0)
    project(col, 1)
    received(h_far[0])
    project(lax.rem(col + 2, 4), 0)
    received(h_rest[1])
    project(left, 1)
    project(right, 1)
    received(h_far[1])
    project(lax.rem(col + 2, 4), 1)
    out[...] = acc[...].astype(bf16)

    for copies in (*z_steps, *v_steps, u_steps, *p_copies, *h_own, *h_rest, *h_far):
        for copy in copies:
            copy.wait_send()


STRIDE = 23
EARLY, MIDDLE, LATE = (1, 7), (2, 6), (3, 5, 4)


def shards(features, short_taps, filter_taps, skip_bias, out_weight):
    tables = [jnp.asarray(t) for t in fourier_tables()]
    near = pl.BlockSpec(memory_space=pltpu.VMEM)
    far = pl.BlockSpec(memory_space=pl.ANY)
    dma, vmem = pltpu.SemaphoreType.DMA, pltpu.VMEM
    return pl.pallas_call(
        kernel,
        out_shape=jax.ShapeDtypeStruct((ROWS, CHAN), bf16),
        in_specs=[far] * 4 + [near] * 7,
        out_specs=near,
        scratch_shapes=[
            vmem((3, ROWS, CHAN), bf16),
            vmem((ROWS, CHAN), f32),
            vmem((4, 2 * ROWS, 2 * ROWS), bf16),
            vmem((3, 16, CHAN), bf16),
            *[vmem((2, CHAN, 128), bf16)] * 6,
            vmem((2, CHAN, 128), f32),
            vmem((SHARE // GROUP, GROUP * BLOCKS, 2 * ROWS), f32),
            vmem((ROWS, CHAN), f32),
            vmem((ROWS, CHAN), f32),
            vmem((4, 8, 2, 64, CHAN), bf16),
            vmem((4, 2, ROWS, WAVE), bf16),
            vmem((ROWS, CHAN), f32),
            dma((3,)),
            pltpu.SemaphoreType.REGULAR((2,)),
            dma((2,)),
            *[dma((2, 2))] * 3,
            dma((2,)),
            *[dma((2, 4))] * 2,
            *[dma((2, 8))] * 2,
            *[dma((8,))] * 2,
            *[dma((4, 8))] * 2,
            *[dma((2, 6))] * 2,
        ],
        compiler_params=pltpu.CompilerParams(
            collective_id=0, has_side_effects=True, vmem_limit_bytes=60 * 1024 * 1024
        ),
    )(
        features, filter_taps, out_weight.T, tables[5],
        short_taps, skip_bias[None, :], *tables[:5],
    )


def solution(mesh):
    placed = (P(None, "seq", "ch"), P(None, None, "ch"), P("seq", "ch"), P("ch"), P("ch", "seq"))
    return jax.shard_map(
        shards, mesh=mesh, in_specs=placed, out_specs=P("seq", "ch"), check_vma=False
    )
```
